512 devices in a mesh: dp: 16 (over x, z_hi, core), ctx: 32 (over z_lo, y).
Axes of the slice: x: 4, y: 4, z: 16 (z_hi: 2, z_lo: 8; z = z_hi * 8 + z_lo), core: 2. Of those that a mesh axis runs over, the one named last changes fastest.
Arguments:
- queries: bfloat16 [16, 12288, 1536], P('dp', 'ctx'), may hold values from -160 to 160
- key_rows: bfloat16 [16, 12288, 1536], P('dp', 'ctx'), may hold values from -8 to 8
- value_rows: bfloat16 [16, 12288, 1536], P('dp', 'ctx'), may hold values from -6 to 6
- tile_lists: int32 [16, 32, 5], P('dp', 'ctx'), may hold values from 0 to 31, as said below
- tile_counts: int32 [16, 32], P('dp', 'ctx'), may hold values from 1 to 5
- out_weight: bfloat16 [1536, 1536], P('dp'), may hold values from -0.15625 to 0.15625
Outputs:
- projected: bfloat16 [16, 12288, 1536], P('dp', 'ctx')
The draws below stay inside these ranges and needn't reach their ends.
Inputs may be any that keep to these rules, and one draw needn't show every extreme that they name: For s < tile_counts[b, t], tile_lists[b, t, s] are distinct tiles of the video within 2 of t, increasing, and t is among them; later slots hold t.
All inputs are finite; a program needn't handle non-finite values.
Results may differ from the reference program's by a relative error of at most 0.0056.
Values may be sent and summed in bfloat16 or wider, within the bound.
No kernel may reach another device: no remote copies, remote signals or barrier semaphores. Data moves between devices by JAX's collectives and lax.ppermute only.
A program may use at most 64 MiB of HBM per device.

```python
import math
import jax
import jax.numpy as jnp
from jax import lax

TILE = 384
HEADS = 12
HD = 128
DOUT = 1536
REACH = 2
SLOTS = 5
NT = 32
VIDEOS = 16
TOKENS = 12288


def window_plan(key):
    base_key = jax.random.fold_in(key, 7)
    bits = jax.random.randint(jax.random.fold_in(base_key, 1), (VIDEOS, NT, SLOTS), 0, 2)
    offsets = jnp.arange(SLOTS, dtype=jnp.int32)[None, None, :] - REACH
    tile_ids = jnp.arange(NT, dtype=jnp.int32)[None, :, None]
    targets = tile_ids + offsets
    full_tile = jax.random.randint(jax.random.fold_in(base_key, 2), (VIDEOS,), REACH, NT - REACH)
    lone_tile = jax.random.randint(jax.random.fold_in(base_key, 3), (VIDEOS,), 0, NT)
    lone_tile = jnp.where(lone_tile == full_tile, (full_tile + 1) % NT, lone_tile)
    chosen = jnp.where(tile_ids == full_tile[:, None, None], 1, bits)
    chosen = jnp.where(tile_ids == lone_tile[:, None, None], 0, chosen)
    chosen = jnp.where(offsets == 0, 1, chosen)
    chosen = jnp.where((targets >= 0) & (targets < NT), chosen, 0)
    order_keys = jnp.where(chosen == 1, offsets, offsets + 4 * SLOTS)
    order = jnp.argsort(order_keys, axis=-1, stable=True)
    sorted_offsets = jnp.take_along_axis(jnp.broadcast_to(offsets, chosen.shape), order, axis=-1)
    counted = jnp.sum(chosen, axis=-1)
    slot_ids = jnp.arange(SLOTS, dtype=jnp.int32)[None, None, :]
    lists = jnp.where(slot_ids < counted[..., None], tile_ids + sorted_offsets, tile_ids)
    return (lists.astype(jnp.int32), counted.astype(jnp.int32))


def draw_tile_lists(key, part):
    return window_plan(key)[0]


def draw_tile_counts(key, part):
    return window_plan(key)[1]


def shaped_keys(key):
    sampled = jax.random.normal(jax.random.fold_in(key, 23), (VIDEOS, TOKENS, HEADS, HD), jnp.float32)
    return jnp.clip(sampled, -8.0, 8.0)


def draw_key_rows(key, part):
    return shaped_keys(key).reshape(VIDEOS, TOKENS, HEADS * HD).astype(jnp.bfloat16)


def draw_queries(key, part):
    sampled = jax.random.normal(jax.random.fold_in(key, 31), (VIDEOS, TOKENS, HEADS, HD), jnp.float32)
    sampled = jnp.clip(sampled, -160.0, 160.0)
    return sampled.reshape(VIDEOS, TOKENS, HEADS * HD).astype(jnp.bfloat16)


def block_scale(rng, dims, pieces, least, high):
    gain, own = 1.0, jax.random.fold_in(rng, 6)
    for axis_at, shards_of in pieces:
        heights = jnp.exp(jax.random.uniform(jax.random.fold_in(own, axis_at), (shards_of,), jnp.float32, least / len(pieces), high / len(pieces)))
        gain = gain * jnp.repeat(heights, dims[axis_at] // shards_of).reshape([-1 if axis == axis_at else 1 for axis in range(len(dims))])
    return gain


def bell_draw(key, extent, scale, bound, pieces=(), kind=jnp.bfloat16):
    entries = jax.random.normal(key, extent, jnp.float32) * scale
    if len(pieces) > 0:
        entries = block_scale(key, extent, pieces, -0.22, 0.18) * entries
    return jnp.clip(entries, min=-bound, max=bound).astype(kind)


def setup_inputs(seed: int = 0) -> dict:
    splits = jax.random.split(jax.random.key(seed), 7)
    queries = draw_queries(jax.random.fold_in(splits[6], 71), 0)
    key_rows = draw_key_rows(jax.random.fold_in(splits[6], 71), 0)
    value_rows = bell_draw(splits[2], (VIDEOS, TOKENS, HEADS * HD), 1.0, 6.0, ((0, 16), (1, 32)))
    tile_lists = draw_tile_lists(jax.random.fold_in(splits[6], 71), 0)
    tile_counts = draw_tile_counts(jax.random.fold_in(splits[6], 71), 0)
    out_weight = bell_draw(splits[5], (HEADS * HD, DOUT), (HEADS * HD) ** -0.5, 0.15625, ((0, 16),))
    return {"queries": queries, "key_rows": key_rows, "value_rows": value_rows, "tile_lists": tile_lists, "tile_counts": tile_counts, "out_weight": out_weight}


def window_mask(tile_lists, tile_counts):
    tile_ids = jnp.arange(NT, dtype=jnp.int32)[None, :, None, None]
    offsets = jnp.arange(SLOTS, dtype=jnp.int32)[None, None, None, :] - REACH
    in_use = (jnp.arange(SLOTS, dtype=jnp.int32)[None, None, :] < tile_counts[:, :, None])[..., None]
    matches = (tile_lists[..., None] == tile_ids + offsets) & in_use
    return jnp.any(matches, axis=2).astype(jnp.int32)

def attend(query_tile, key_window, value_window, visible_tiles):
    query_heads = query_tile.reshape(TILE, HEADS, HD).astype(jnp.float32)
    key_heads = key_window.reshape(SLOTS * TILE, HEADS, HD).astype(jnp.float32)
    value_heads = value_window.reshape(SLOTS * TILE, HEADS, HD).astype(jnp.float32)
    scores = jnp.einsum('thd,khd->htk', query_heads, key_heads, precision=lax.Precision.HIGHEST) * (1.0 / math.sqrt(HD))
    expanded = (jnp.repeat(visible_tiles, TILE) > 0)[None, None, :]
    peak_rows = lax.optimization_barrier(jnp.max(jnp.where(expanded, scores, jnp.float32(-1e+30)), axis=-1, keepdims=True))
    exponent = jnp.where(expanded, jnp.exp(scores - peak_rows), jnp.float32(0.0))
    totals = lax.optimization_barrier(jnp.sum(exponent, axis=-1))
    probs = exponent.astype(jnp.bfloat16)
    mixture = jnp.einsum('htk,khd->htd', probs.astype(jnp.float32), value_heads, precision=lax.Precision.HIGHEST)
    result = (mixture / totals[..., None]).astype(jnp.bfloat16)
    return result.transpose(1, 0, 2).reshape(TILE, HEADS * HD)

def reference(queries, key_rows, value_rows, tile_lists, tile_counts, out_weight):
    visible = window_mask(tile_lists, tile_counts)
    padding = jnp.zeros((REACH * TILE, HEADS * HD), jnp.bfloat16)

    def one_video(video_pos):
        query_block = queries[video_pos]
        key_block = jnp.concatenate([padding, key_rows[video_pos], padding], axis=0)
        value_block = jnp.concatenate([padding, value_rows[video_pos], padding], axis=0)
        visible_video = visible[video_pos]

        def one_tile(tile_pos):
            query_tile = lax.dynamic_slice_in_dim(query_block, tile_pos * TILE, TILE, 0)
            key_window = lax.dynamic_slice_in_dim(key_block, tile_pos * TILE, SLOTS * TILE, 0)
            value_window = lax.dynamic_slice_in_dim(value_block, tile_pos * TILE, SLOTS * TILE, 0)
            return attend(query_tile, key_window, value_window, visible_video[tile_pos])
        return lax.map(one_tile, jnp.arange(NT, dtype=jnp.int32)).reshape(TOKENS, HEADS * HD)
    attention = lax.map(one_video, jnp.arange(VIDEOS, dtype=jnp.int32))
    result = jnp.dot(attention.reshape(VIDEOS * TOKENS, HEADS * HD), out_weight, preferred_element_type=jnp.float32)
    return result.astype(jnp.bfloat16).reshape(VIDEOS, TOKENS, DOUT)
```

```python
import math

import jax
import jax.numpy as jnp
from jax import lax
from jax.experimental import pallas as pl
from jax.experimental.pallas import tpu as pltpu
from jax.sharding import PartitionSpec as P

HD = 128
SLOTS = 5
TILE = 384
DOUT = 1536
RING = 4
RUNS = 8
HEADS_HERE = 3
GC = HEADS_HERE * HD
EXTRA = 16
CHUNKS = ((0, 2), (2, 1))
FACTOR = math.log2(math.e) / math.sqrt(HD)
VMEM = 100 * 1024 * 1024 // 2


def z_pairs(by):
    return [
        (z * RING + y, (z + by) * RING + y)
        for z in range(RUNS)
        for y in range(RING)
        if 0 <= z + by < RUNS
    ]


def mirror_pairs():
    pairs = []
    for x in range(4):
        for high in range(2):
            for core in range(2):
                for z in range(RUNS):
                    for y in range(RING):
                        here = (x * 4 + high * 2 + core) * 32 + z * RING + y
                        there = (x * 4 + (1 - high) * 2 + core) * 32 + (RUNS - 1 - z) * RING + y
                        pairs.append((here, there))
    return pairs


def call(kernel, name, outs, scratch, flops, nbytes, smem):
    any_spec = pl.BlockSpec(memory_space=pl.ANY)

    def run(*args):
        specs = [
            pl.BlockSpec(memory_space=pltpu.SMEM) if i < smem else any_spec
            for i in range(len(args))
        ]
        return pl.pallas_call(
            kernel,
            out_shape=outs,
            in_specs=specs,
            out_specs=jax.tree.map(lambda _: any_spec, outs),
            scratch_shapes=scratch,
            compiler_params=pltpu.CompilerParams(vmem_limit_bytes=VMEM),
            cost_estimate=pl.CostEstimate(flops=flops, bytes_accessed=nbytes, transcendentals=0),
            name=name,
        )(*args)

    return run


def pack_kernel(sources, *refs):
    ins, out, sems = refs[:sources], refs[sources], refs[-1]
    copies = []
    for at in range(RING):
        for i, ref in enumerate(ins):
            copies.append(
                pltpu.make_async_copy(
                    ref.at[0, :, pl.ds(at * GC, GC)],
                    out.at[at, i, pl.ds(0, TILE)],
                    sems.at[len(copies)],
                )
            )
            copies[-1].start()
    for copy in copies:
        copy.wait()


def pack(*arrays):
    count = len(arrays)
    return call(
        lambda *refs: pack_kernel(count, *refs),
        "pack",
        jax.ShapeDtypeStruct((RING, count, TILE, GC), jnp.bfloat16),
        [pltpu.SemaphoreType.DMA((RING * count,))],
        0,
        count * TILE * DOUT * 4,
        0,
    )(*arrays)


def pack_plan_kernel(source, plan, out, sems):
    copies = []
    for at in range(RING):
        for part in (
            (source.at[0, :, pl.ds(at * GC, GC)], out.at[at, pl.ds(0, TILE)]),
            (plan, out.at[at, pl.ds(TILE, EXTRA)]),
        ):
            copies.append(pltpu.make_async_copy(*part, sems.at[len(copies)]))
            copies[-1].start()
    for copy in copies:
        copy.wait()


def pack_plan(array, plan):
    return call(
        pack_plan_kernel,
        "pack_plan",
        jax.ShapeDtypeStruct((RING, TILE + EXTRA, GC), jnp.bfloat16),
        [pltpu.SemaphoreType.DMA((RING * 2,))],
        0,
        TILE * DOUT * 4,
        0,
    )(array, plan)


def attend_kernel(first, heads, lists, *refs):
    q_in, kv_in, before, after, out, qb, kvb, ob, in_sems, out_sems = refs
    wide = heads * HD
    columns = pl.ds(first * HD, wide)
    y = lax.rem(lax.axis_index("ctx"), RING)
    base = lax.axis_index("ctx") - y
    copies = []
    for source, target in (
        (q_in.at[:, pl.ds(0, TILE), columns], qb),
        (kv_in.at[:, :, :, columns], kvb.at[pl.ds(0, 4)]),
        (before.at[:, :, :, columns], kvb.at[pl.ds(4, 2)]),
        (after.at[:, :, :, columns], kvb.at[pl.ds(6, 2)]),
    ):
        copies.append(pltpu.make_async_copy(source, target, in_sems.at[len(copies)]))
        copies[-1].start()
    for copy in copies:
        copy.wait()
    ones = jnp.ones((TILE, HD), jnp.bfloat16)

    def body(step, carry):
        at = lax.rem(step, RING)
        col = pl.ds(pl.multiple_of(lax.div(step, RING) * HD, HD), HD)
        live = lists[at, SLOTS]
        for count in range(1, SLOTS + 1):

            @pl.when(live == count)
            def _():
                slots = []
                for s in range(count):
                    tile = lists[at, s] - base
                    slots.append(tile + jnp.where(tile < 0, 6, jnp.where(tile < RING, 0, 2)))
                query = qb[at, :, col]
                scores = [
                    lax.dot_general(
                        query,
                        kvb[slot, 0, :, col],
                        (((1,), (1,)), ((), ())),
                        preferred_element_type=jnp.float32,
                    )
                    for slot in slots
                ]
                high = scores[0]
                for score in scores[1:]:
                    high = jnp.maximum(high, score)
                peak = jnp.max(high, axis=1, keepdims=True)
                total = jnp.zeros((TILE, 2 * HD), jnp.float32)
                for slot, score in zip(slots, scores):
                    probs = jnp.exp2((score - peak) * FACTOR).astype(jnp.bfloat16)
                    value = jnp.concatenate([kvb[slot, 1, :, col], ones], axis=1)
                    total += jnp.dot(probs, value, preferred_element_type=jnp.float32)
                ob[at, :, col] = (total[:, :HD] / total[:, HD:]).astype(jnp.bfloat16)

        return carry

    lax.fori_loop(0, RING * heads, body, 0)
    last = pltpu.make_async_copy(ob, out, out_sems.at[0])
    last.start()
    last.wait()


def attend(first, heads, lists, *arrays):
    wide = heads * HD
    return call(
        lambda *refs: attend_kernel(first, heads, *refs),
        f"attend{first}",
        jax.ShapeDtypeStruct((RING, TILE, wide), jnp.bfloat16),
        [
            pltpu.VMEM((RING, TILE, wide), jnp.bfloat16),
            pltpu.VMEM((2 * RING, 2, TILE, wide), jnp.bfloat16),
            pltpu.VMEM((RING, TILE, wide), jnp.bfloat16),
            pltpu.SemaphoreType.DMA((4,)),
            pltpu.SemaphoreType.DMA((1,)),
        ],
        heads * 5_000_000_000,
        heads * 1_600_000,
        1,
    )(lists, *arrays)


def project(weight, parts):
    def kernel(*refs):
        ins, (own_in, other_in, out, rows, weights, result, sems) = refs[: len(parts)], refs[len(parts) :]
        high = lax.rem(lax.div(lax.axis_index("dp"), 2), 2)
        copies = []

        def copy(source, target):
            copies.append(pltpu.make_async_copy(source, target, sems.at[len(copies)]))
            copies[-1].start()

        for ref, half in ((own_in, high), (other_in, 1 - high)):
            for pair in range(8):
                place = ((pair // 2) * 4 + half * 2 + pair % 2) * 96
                copy(
                    ref.at[pl.ds(pair * 96, 96)],
                    weights.at[pl.ds(pl.multiple_of(place, 96), 96)],
                )
        for ref, (first, heads) in zip(ins, CHUNKS):
            for g in range(RING):
                copy(ref.at[g], rows.at[:, pl.ds(g * GC + first * HD, heads * HD)])
        for each in copies:
            each.wait()

        def body(step, carry):
            col = pl.ds(pl.multiple_of(step * 512, 512), 512)
            result[:, col] = jnp.dot(
                rows[...], weights[:, col], preferred_element_type=jnp.float32
            ).astype(jnp.bfloat16)
            return carry

        lax.fori_loop(0, DOUT // 512, body, 0)
        last = pltpu.make_async_copy(result, out.at[0], sems.at[len(copies)])
        last.start()
        last.wait()

    return call(
        kernel,
        "project",
        jax.ShapeDtypeStruct((1, TILE, DOUT), jnp.bfloat16),
        [
            pltpu.VMEM((TILE, DOUT), jnp.bfloat16),
            pltpu.VMEM((DOUT, DOUT), jnp.bfloat16),
            pltpu.VMEM((TILE, DOUT), jnp.bfloat16),
            pltpu.SemaphoreType.DMA((16 + RING * len(parts) + 1,)),
        ],
        2 * TILE * DOUT * DOUT,
        8_000_000,
        0,
    )(*parts, *weight)


def per_device(queries, key_rows, value_rows, tile_lists, tile_counts, out_weight):
    groups = [[z * RING + y for y in range(RING)] for z in range(RUNS)]
    fours = [[x * 4 + high * 2 + core for x in range(4) for core in range(2)] for high in range(2)]

    def exchange(value):
        return lax.all_to_all(value, "ctx", 0, 0, axis_index_groups=groups)

    def gather(value):
        return lax.all_gather(value, "dp", axis=0, tiled=True, axis_index_groups=fours)

    kv = pack(key_rows, value_rows)
    other = lax.ppermute(out_weight, ("dp", "ctx"), mirror_pairs())
    weight = gather(out_weight), gather(other)
    plan = jnp.concatenate([tile_lists[0], tile_counts], axis=1).astype(jnp.bfloat16)
    plan = jnp.pad(plan, ((0, EXTRA - 1), (0, GC - SLOTS - 1)))
    query = pack_plan(queries, plan)
    kv = exchange(kv)
    before = lax.ppermute(kv[2:], "ctx", z_pairs(1))
    after = lax.ppermute(kv[:2], "ctx", z_pairs(-1))
    query = exchange(query)
    lists = query[:, TILE, :8].astype(jnp.int32)
    parts = []
    for first, heads in CHUNKS:
        parts.append(exchange(attend(first, heads, lists, query, kv, before, after)))
    return project(weight, parts)


def solution(mesh):
    in_specs = (
        P("dp", "ctx", None),
        P("dp", "ctx", None),
        P("dp", "ctx", None),
        P("dp", "ctx", None),
        P("dp", "ctx"),
        P("dp", None),
    )
    out_specs = P("dp", "ctx", None)
    return jax.shard_map(
        per_device, mesh=mesh, in_specs=in_specs, out_specs=out_specs, check_vma=False
    )
```

```python
import math

import jax
import jax.numpy as jnp
from jax import lax
from jax.experimental import pallas as pl
from jax.experimental.pallas import tpu as pltpu
from jax.sharding import PartitionSpec as P

HD = 128
SLOTS = 5
TILE = 384
DOUT = 1536
RING = 4
RUNS = 8
HEADS_HERE = 3
GC = HEADS_HERE * HD
EXTRA = 16
CHUNKS = ((0, 2), (2, 1))
FACTOR = math.log2(math.e) / math.sqrt(HD)
VMEM = 62 * 1024 * 1024


def z_pairs(by):
    return [
        (z * RING + y, (z + by) * RING + y)
        for z in range(RUNS)
        for y in range(RING)
        if 0 <= z + by < RUNS
    ]


def mirror_pairs():
    pairs = []
    for x in range(4):
        for high in range(2):
            for core in range(2):
                for z in range(RUNS):
                    for y in range(RING):
                        here = (x * 4 + high * 2 + core) * 32 + z * RING + y
                        there = (x * 4 + (1 - high) * 2 + core) * 32 + (RUNS - 1 - z) * RING + y
                        pairs.append((here, there))
    return pairs


def call(kernel, name, outs, scratch, flops, nbytes, smem):
    any_spec = pl.BlockSpec(memory_space=pl.ANY)

    def run(*args):
        specs = [
            pl.BlockSpec(memory_space=pltpu.SMEM) if i < smem else any_spec
            for i in range(len(args))
        ]
        return pl.pallas_call(
            kernel,
            out_shape=outs,
            in_specs=specs,
            out_specs=jax.tree.map(lambda _: any_spec, outs),
            scratch_shapes=scratch,
            compiler_params=pltpu.CompilerParams(vmem_limit_bytes=VMEM),
            cost_estimate=pl.CostEstimate(flops=flops, bytes_accessed=nbytes, transcendentals=0),
            name=name,
        )(*args)

    return run


def pack(arrays, plan=None):
    tall = TILE * len(arrays) + (0 if plan is None else EXTRA)
    count = len(arrays)

    def kernel(*refs):
        sources, (out, block, in_sems, out_sems) = refs[:count], refs[-4:]
        loads, stores = [], []
        for i, source in enumerate(sources):
            for at in range(RING):
                n = len(loads)
                loads.append(
                    pltpu.make_async_copy(
                        source.at[0, :, pl.ds(at * GC, GC)], block.at[n], in_sems.at[n]
                    )
                )
                stores.append(
                    pltpu.make_async_copy(
                        block.at[n], out.at[at, pl.ds(i * TILE, TILE)], out_sems.at[n]
                    )
                )
                loads[-1].start()
        if plan is not None:
            for at in range(RING):
                stores.append(
                    pltpu.make_async_copy(
                        refs[count],
                        out.at[at, pl.ds(count * TILE, EXTRA)],
                        out_sems.at[len(stores)],
                    )
                )
                stores[-1].start()
        for load, store in zip(loads, stores):
            load.wait()
            store.start()
        for store in stores:
            store.wait()

    return call(
        kernel,
        f"pack{count}",
        jax.ShapeDtypeStruct((RING, tall, GC), jnp.bfloat16),
        [
            pltpu.VMEM((RING * count, TILE, GC), jnp.bfloat16),
            pltpu.SemaphoreType.DMA((RING * count,)),
            pltpu.SemaphoreType.DMA((RING * (count + 1),)),
        ],
        0,
        RING * tall * GC * 4,
        0,
    )(*arrays, *([] if plan is None else [plan]))


def attend_kernel(first, heads, lists, *refs):
    kv_in, q_in, before, after, out, qb, kvb, ob, in_sems, out_sems = refs
    columns = pl.ds(first * HD, heads * HD)
    base = lax.div(lax.axis_index("ctx"), RING) * RING
    copies = []
    for source, target in (
        (q_in.at[:, pl.ds(0, TILE), columns], qb),
        (kv_in.at[:, :, columns], kvb.at[pl.ds(0, 4)]),
        (before.at[:, :, columns], kvb.at[pl.ds(4, 2)]),
        (after.at[:, :, columns], kvb.at[pl.ds(6, 2)]),
    ):
        copies.append(pltpu.make_async_copy(source, target, in_sems.at[len(copies)]))
        copies[-1].start()
    for copy in copies:
        copy.wait()
    half = TILE // 2

    def tile_of(at, count):
        slots = []
        for s in range(count):
            tile = lists[at, s] - base
            slots.append(tile + jnp.where(tile < 0, 6, jnp.where(tile < RING, 0, 2)))

        def column_of(part, col):
            return jnp.concatenate(
                [kvb[slot, pl.ds(part * TILE, TILE), col] for slot in slots], axis=0
            )

        def score(rows, col):
            scores = lax.dot_general(
                qb[at, rows, col],
                column_of(0, col),
                (((1,), (1,)), ((), ())),
                preferred_element_type=jnp.float32,
            )
            return scores, jnp.max(scores, axis=1, keepdims=True)

        def mix(rows, col, scores, peak):
            probs = jnp.exp2((scores - peak) * FACTOR).astype(jnp.bfloat16)
            ones = jnp.ones((count * TILE, HD), jnp.bfloat16)
            value = jnp.concatenate([column_of(1, col), ones], axis=1)
            total = jnp.dot(probs, value, preferred_element_type=jnp.float32)
            ob[at, rows, col] = (total[:, :HD] / total[:, HD:]).astype(jnp.bfloat16)

        for head in range(heads):
            col = pl.ds(head * HD, HD)
            upper, lower = pl.ds(0, half), pl.ds(half, half)
            first_scores = score(upper, col)
            second_scores = score(lower, col)
            mix(upper, col, *first_scores)
            mix(lower, col, *second_scores)

    def body(at, carry):
        live = lists[at, SLOTS]
        for count in range(1, SLOTS + 1):

            @pl.when(live == count)
            def _():
                tile_of(at, count)

        return carry

    lax.fori_loop(0, RING, body, 0)
    last = pltpu.make_async_copy(ob, out, out_sems.at[0])
    last.start()
    last.wait()


def attend(first, heads, lists, *arrays):
    wide = heads * HD
    return call(
        lambda *refs: attend_kernel(first, heads, *refs),
        f"attend{first}",
        jax.ShapeDtypeStruct((RING, TILE, wide), jnp.bfloat16),
        [
            pltpu.VMEM((RING, TILE, wide), jnp.bfloat16),
            pltpu.VMEM((2 * RING, 2 * TILE, wide), jnp.bfloat16),
            pltpu.VMEM((RING, TILE, wide), jnp.bfloat16),
            pltpu.SemaphoreType.DMA((4,)),
            pltpu.SemaphoreType.DMA((1,)),
        ],
        heads * 5_000_000_000,
        heads * 1_600_000,
        1,
    )(lists, *arrays)


def project(first, heads, part, near, far, total=None):
    wide = heads * HD
    deep = RING * wide
    pieces = []
    for shard in range(4):
        low, high = max(shard * 96, first * HD), min(shard * 96 + 96, first * HD + wide)
        if low < high:
            pieces.append((low - first * HD, high - low, shard % 2, shard // 2, low - shard * 96))

    def kernel(*refs):
        part_in, near_in, far_in, *others = refs
        if total is None:
            out, rows, weights, result, sems = others
        else:
            total_in, out, rows, weights, result, sums, sems = others
        z_half = lax.rem(lax.div(lax.axis_index("dp"), 2), 2)

        def weight_copies(own):
            copies = []
            for g in range(RING):
                for to, count, core, half, at in pieces:
                    source = near_in if half == own else far_in
                    copies.append(
                        pltpu.make_async_copy(
                            source.at[pl.ds((2 * g + core) * 96 + at, count)],
                            weights.at[pl.ds(g * wide + to, count)],
                            sems.at[len(copies)],
                        )
                    )
            return copies

        for own in range(2):

            @pl.when(z_half == own)
            def _():
                for copy in weight_copies(own):
                    copy.start()

        waits = weight_copies(0)
        for g in range(RING):
            copy = pltpu.make_async_copy(
                part_in.at[g], rows.at[:, pl.ds(g * wide, wide)], sems.at[len(waits)]
            )
            copy.start()
            waits.append(copy)
        if total is not None:
            copy = pltpu.make_async_copy(total_in, sums, sems.at[len(waits)])
            copy.start()
            waits.append(copy)
        for copy in waits:
            copy.wait()
        stores = []
        for step in range(DOUT // 512):
            col = pl.ds(step * 512, 512)
            product = jnp.dot(rows[...], weights[:, col], preferred_element_type=jnp.float32)
            if total is not None:
                product = (product + sums[:, col]).astype(jnp.bfloat16)
            result[:, col] = product
            target = out.at[:, col] if total is None else out.at[0, :, col]
            stores.append(pltpu.make_async_copy(result.at[:, col], target, sems.at[step]))
            stores[-1].start()
        for store in stores:
            store.wait()

    kind = jnp.float32 if total is None else jnp.bfloat16
    shape = (TILE, DOUT) if total is None else (1, TILE, DOUT)
    scratch = [
        pltpu.VMEM((TILE, deep), jnp.bfloat16),
        pltpu.VMEM((deep, DOUT), jnp.bfloat16),
        pltpu.VMEM((TILE, DOUT), kind),
    ]
    if total is not None:
        scratch.append(pltpu.VMEM((TILE, DOUT), jnp.float32))
    scratch.append(pltpu.SemaphoreType.DMA((RING * len(pieces) + RING + 1,)))
    return call(
        kernel,
        f"project{first}",
        jax.ShapeDtypeStruct(shape, kind),
        scratch,
        2 * TILE * deep * DOUT,
        8_000_000,
        0,
    )(part, near, far, *([] if total is None else [total]))


def per_device(queries, key_rows, value_rows, tile_lists, tile_counts, out_weight):
    groups = [[z * RING + y for y in range(RING)] for z in range(RUNS)]
    pairs = [[x * 4 + high * 2 + core for x in range(4) for core in range(2)] for high in range(2)]

    def exchange(value):
        return lax.all_to_all(value, "ctx", 0, 0, axis_index_groups=groups)

    def gather(value):
        return lax.all_gather(value, "dp", axis=0, tiled=True, axis_index_groups=pairs)

    def halo(value):
        return (
            lax.ppermute(value[2:], "ctx", z_pairs(1)),
            lax.ppermute(value[:2], "ctx", z_pairs(-1)),
        )

    def after(values, done):
        return lax.optimization_barrier((values, done))[0]

    packed = pack((key_rows, value_rows))
    out_weight, queries, tile_lists, tile_counts = after(
        (out_weight, queries, tile_lists, tile_counts), packed
    )
    plan = jnp.concatenate([tile_lists[0], tile_counts], axis=1).astype(jnp.bfloat16)
    plan = jnp.pad(plan, ((0, EXTRA - 1), (0, GC - SLOTS - 1)))
    near = gather(out_weight)
    other = lax.ppermute(out_weight, ("dp", "ctx"), mirror_pairs())
    key_values = exchange(packed)
    packed, key_values, other = lax.optimization_barrier(
        (pack((queries,), plan), key_values, other)
    )
    far = gather(other)
    query = exchange(packed)
    edges = halo(key_values)
    lists = query[:, TILE, :8].astype(jnp.int32)
    query, edges = lax.optimization_barrier((query, edges))
    parts = []
    for first, heads in CHUNKS:
        mixed = attend(first, heads, lists, key_values, query, *edges)
        if parts:
            mixed, parts[-1] = lax.optimization_barrier((mixed, parts[-1]))
        else:
            mixed, query = lax.optimization_barrier((mixed, query))
        parts.append(exchange(mixed))
    total = project(*CHUNKS[0], parts[0], near, far)
    return project(*CHUNKS[1], parts[1], near, far, total)


def solution(mesh):
    in_specs = (
        P("dp", "ctx", None),
        P("dp", "ctx", None),
        P("dp", "ctx", None),
        P("dp", "ctx", None),
        P("dp", "ctx"),
        P("dp", None),
    )
    out_specs = P("dp", "ctx", None)
    return jax.shard_map(
        per_device, mesh=mesh, in_specs=in_specs, out_specs=out_specs, check_vma=False
    )
```

```python
import math

import jax
import jax.numpy as jnp
from jax import lax
from jax.experimental import pallas as pl
from jax.experimental.pallas import tpu as pltpu
from jax.sharding import PartitionSpec as P

HD = 128
SLOTS = 5
TILE = 384
DOUT = 1536
RING = 4
RUNS = 8
HEADS_HERE = 3
GC = HEADS_HERE * HD
EXTRA = 16
CHUNKS = ((0, HEADS_HERE),)
FACTOR = math.log2(math.e) / math.sqrt(HD)
VMEM = 62 * 1024 * 1024


def z_pairs(by):
    return [
        (z * RING + y, (z + by) * RING + y)
        for z in range(RUNS)
        for y in range(RING)
        if 0 <= z + by < RUNS
    ]


def mirror_pairs():
    pairs = []
    for x in range(4):
        for high in range(2):
            for core in range(2):
                for z in range(RUNS):
                    for y in range(RING):
                        here = (x * 4 + high * 2 + core) * 32 + z * RING + y
                        there = (x * 4 + (1 - high) * 2 + core) * 32 + (RUNS - 1 - z) * RING + y
                        pairs.append((here, there))
    return pairs


def call(kernel, name, outs, scratch, flops, nbytes, smem):
    any_spec = pl.BlockSpec(memory_space=pl.ANY)

    def run(*args):
        specs = [
            pl.BlockSpec(memory_space=pltpu.SMEM) if i < smem else any_spec
            for i in range(len(args))
        ]
        return pl.pallas_call(
            kernel,
            out_shape=outs,
            in_specs=specs,
            out_specs=jax.tree.map(lambda _: any_spec, outs),
            scratch_shapes=scratch,
            compiler_params=pltpu.CompilerParams(vmem_limit_bytes=VMEM),
            cost_estimate=pl.CostEstimate(flops=flops, bytes_accessed=nbytes, transcendentals=0),
            name=name,
        )(*args)

    return run


def pack(arrays, plan=None):
    tall = TILE * len(arrays) + (0 if plan is None else EXTRA)
    count = len(arrays)

    def kernel(*refs):
        sources, (out, block, in_sems, out_sems) = refs[:count], refs[-4:]
        loads, stores = [], []
        for i, source in enumerate(sources):
            for at in range(RING):
                n = len(loads)
                loads.append(
                    pltpu.make_async_copy(
                        source.at[0, :, pl.ds(at * GC, GC)], block.at[n], in_sems.at[n]
                    )
                )
                stores.append(
                    pltpu.make_async_copy(
                        block.at[n], out.at[at, pl.ds(i * TILE, TILE)], out_sems.at[n]
                    )
                )
                loads[-1].start()
        if plan is not None:
            for at in range(RING):
                stores.append(
                    pltpu.make_async_copy(
                        refs[count],
                        out.at[at, pl.ds(count * TILE, EXTRA)],
                        out_sems.at[len(stores)],
                    )
                )
                stores[-1].start()
        for load, store in zip(loads, stores):
            load.wait()
            store.start()
        for store in stores:
            store.wait()

    return call(
        kernel,
        f"pack{count}",
        jax.ShapeDtypeStruct((RING, tall, GC), jnp.bfloat16),
        [
            pltpu.VMEM((RING * count, TILE, GC), jnp.bfloat16),
            pltpu.SemaphoreType.DMA((RING * count,)),
            pltpu.SemaphoreType.DMA((RING * (count + 1),)),
        ],
        0,
        RING * tall * GC * 4,
        0,
    )(*arrays, *([] if plan is None else [plan]))


def attend_kernel(first, heads, lists, *refs):
    kv_in, q_in, before, after, out, qb, kvb, ob, in_sems, out_sems = refs
    columns = pl.ds(first * HD, heads * HD)
    base = lax.div(lax.axis_index("ctx"), RING) * RING
    copies = []
    for source, target in (
        (q_in.at[:, pl.ds(0, TILE), columns], qb),
        (kv_in.at[:, :, columns], kvb.at[pl.ds(0, 4)]),
        (before.at[:, :, columns], kvb.at[pl.ds(4, 2)]),
        (after.at[:, :, columns], kvb.at[pl.ds(6, 2)]),
    ):
        copies.append(pltpu.make_async_copy(source, target, in_sems.at[len(copies)]))
        copies[-1].start()
    for copy in copies:
        copy.wait()
    half = TILE // 2

    def tile_of(at, count):
        slots = []
        for s in range(count):
            tile = lists[at, s] - base
            slots.append(tile + jnp.where(tile < 0, 6, jnp.where(tile < RING, 0, 2)))

        def column_of(part, col):
            return jnp.concatenate(
                [kvb[slot, pl.ds(part * TILE, TILE), col] for slot in slots], axis=0
            )

        def score(rows, col):
            scores = lax.dot_general(
                qb[at, rows, col],
                column_of(0, col),
                (((1,), (1,)), ((), ())),
                preferred_element_type=jnp.float32,
            )
            return scores, jnp.max(scores, axis=1, keepdims=True)

        def mix(rows, col, scores, peak):
            probs = jnp.exp2((scores - peak) * FACTOR).astype(jnp.bfloat16)
            ones = jnp.ones((count * TILE, HD), jnp.bfloat16)
            value = jnp.concatenate([column_of(1, col), ones], axis=1)
            total = jnp.dot(probs, value, preferred_element_type=jnp.float32)
            ob[at, rows, col] = (total[:, :HD] / total[:, HD:]).astype(jnp.bfloat16)

        for head in range(heads):
            col = pl.ds(head * HD, HD)
            upper, lower = pl.ds(0, half), pl.ds(half, half)
            first_scores = score(upper, col)
            second_scores = score(lower, col)
            mix(upper, col, *first_scores)
            mix(lower, col, *second_scores)

    def body(at, carry):
        live = lists[at, SLOTS]
        for count in range(1, SLOTS + 1):

            @pl.when(live == count)
            def _():
                tile_of(at, count)

        return carry

    lax.fori_loop(0, RING, body, 0)
    last = pltpu.make_async_copy(ob, out, out_sems.at[0])
    last.start()
    last.wait()


def attend(first, heads, lists, *arrays):
    wide = heads * HD
    return call(
        lambda *refs: attend_kernel(first, heads, *refs),
        f"attend{first}",
        jax.ShapeDtypeStruct((RING, TILE, wide), jnp.bfloat16),
        [
            pltpu.VMEM((RING, TILE, wide), jnp.bfloat16),
            pltpu.VMEM((2 * RING, 2 * TILE, wide), jnp.bfloat16),
            pltpu.VMEM((RING, TILE, wide), jnp.bfloat16),
            pltpu.SemaphoreType.DMA((4,)),
            pltpu.SemaphoreType.DMA((1,)),
        ],
        heads * 5_000_000_000,
        heads * 1_600_000,
        1,
    )(lists, *arrays)


def project(first, heads, part, near, far):
    wide = heads * HD
    deep = RING * wide
    pieces = []
    for shard in range(4):
        low, high = max(shard * 96, first * HD), min(shard * 96 + 96, first * HD + wide)
        if low < high:
            pieces.append((low - first * HD, high - low, shard % 2, shard // 2, low - shard * 96))

    def kernel(*refs):
        part_in, near_in, far_in, *others = refs
        out, rows, weights, result, sems = others
        z_half = lax.rem(lax.div(lax.axis_index("dp"), 2), 2)

        def weight_copies(own):
            copies = []
            for g in range(RING):
                for to, count, core, half, at in pieces:
                    source = near_in if half == own else far_in
                    copies.append(
                        pltpu.make_async_copy(
                            source.at[pl.ds((2 * g + core) * 96 + at, count)],
                            weights.at[pl.ds(g * wide + to, count)],
                            sems.at[len(copies)],
                        )
                    )
            return copies

        for own in range(2):

            @pl.when(z_half == own)
            def _():
                for copy in weight_copies(own):
                    copy.start()

        waits = weight_copies(0)
        for g in range(RING):
            copy = pltpu.make_async_copy(
                part_in.at[g], rows.at[:, pl.ds(g * wide, wide)], sems.at[len(waits)]
            )
            copy.start()
            waits.append(copy)
        for copy in waits:
            copy.wait()
        stores = []
        for step in range(DOUT // 512):
            col = pl.ds(step * 512, 512)
            product = jnp.dot(rows[...], weights[:, col], preferred_element_type=jnp.float32)
            result[:, col] = product.astype(jnp.bfloat16)
            target = out.at[0, :, col]
            stores.append(pltpu.make_async_copy(result.at[:, col], target, sems.at[step]))
            stores[-1].start()
        for store in stores:
            store.wait()

    shape = jax.ShapeDtypeStruct((1, TILE, DOUT), jnp.bfloat16)
    scratch = [
        pltpu.VMEM((TILE, deep), jnp.bfloat16),
        pltpu.VMEM((deep, DOUT), jnp.bfloat16),
        pltpu.VMEM((TILE, DOUT), jnp.bfloat16),
        pltpu.SemaphoreType.DMA((RING * len(pieces) + RING,)),
    ]
    return call(
        kernel,
        f"project{first}",
        shape,
        scratch,
        2 * TILE * deep * DOUT,
        8_000_000,
        0,
    )(part, near, far)


def per_device(queries, key_rows, value_rows, tile_lists, tile_counts, out_weight):
    groups = [[z * RING + y for y in range(RING)] for z in range(RUNS)]
    pairs = [[x * 4 + high * 2 + core for x in range(4) for core in range(2)] for high in range(2)]

    def exchange(value):
        return lax.all_to_all(value, "ctx", 0, 0, axis_index_groups=groups)

    def gather(value):
        return lax.all_gather(value, "dp", axis=0, tiled=True, axis_index_groups=pairs)

    def halo(value):
        return (
            lax.ppermute(value[2:], "ctx", z_pairs(1)),
            lax.ppermute(value[:2], "ctx", z_pairs(-1)),
        )

    def after(values, done):
        return lax.optimization_barrier((values, done))[0]

    packed = pack((key_rows, value_rows))
    out_weight, queries, tile_lists, tile_counts = after(
        (out_weight, queries, tile_lists, tile_counts), packed
    )
    plan = jnp.concatenate([tile_lists[0], tile_counts], axis=1).astype(jnp.bfloat16)
    plan = jnp.pad(plan, ((0, EXTRA - 1), (0, GC - SLOTS - 1)))
    near = gather(out_weight)
    other = lax.ppermute(out_weight, ("dp", "ctx"), mirror_pairs())
    key_values = exchange(packed)
    packed, key_values, other = lax.optimization_barrier(
        (pack((queries,), plan), key_values, other)
    )
    far = gather(other)
    query = exchange(packed)
    edges = halo(key_values)
    lists = query[:, TILE, :8].astype(jnp.int32)
    query, edges = lax.optimization_barrier((query, edges))
    first, heads = CHUNKS[0]
    mixed = attend(first, heads, lists, key_values, query, *edges)
    return project(first, heads, exchange(mixed), near, far)


def solution(mesh):
    in_specs = (
        P("dp", "ctx", None),
        P("dp", "ctx", None),
        P("dp", "ctx", None),
        P("dp", "ctx", None),
        P("dp", "ctx"),
        P("dp", None),
    )
    out_specs = P("dp", "ctx", None)
    return jax.shard_map(
        per_device, mesh=mesh, in_specs=in_specs, out_specs=out_specs, check_vma=False
    )
```

```python
import math

import jax
import jax.numpy as jnp
from jax import lax
from jax.experimental import pallas as pl
from jax.experimental.pallas import tpu as pltpu
from jax.sharding import PartitionSpec as P

HD = 128
SLOTS = 5
TILE = 384
DOUT = 1536
RING = 4
RUNS = 8
HEADS_HERE = 3
GC = HEADS_HERE * HD
EXTRA = 16
CHUNKS = ((0, HEADS_HERE),)
FACTOR = math.log2(math.e) / math.sqrt(HD)
VMEM = 62 * 1024 * 1024


def z_pairs(by):
    return [
        (z * RING + y, (z + by) * RING + y)
        for z in range(RUNS)
        for y in range(RING)
        if 0 <= z + by < RUNS
    ]


def mirror_pairs():
    pairs = []
    for x in range(4):
        for high in range(2):
            for core in range(2):
                for z in range(RUNS):
                    for y in range(RING):
                        here = (x * 4 + high * 2 + core) * 32 + z * RING + y
                        there = (x * 4 + (1 - high) * 2 + core) * 32 + (RUNS - 1 - z) * RING + y
                        pairs.append((here, there))
    return pairs


def call(kernel, name, outs, scratch, flops, nbytes, smem):
    any_spec = pl.BlockSpec(memory_space=pl.ANY)

    def run(*args):
        specs = [
            pl.BlockSpec(memory_space=pltpu.SMEM) if i < smem else any_spec
            for i in range(len(args))
        ]
        return pl.pallas_call(
            kernel,
            out_shape=outs,
            in_specs=specs,
            out_specs=jax.tree.map(lambda _: any_spec, outs),
            scratch_shapes=scratch,
            compiler_params=pltpu.CompilerParams(vmem_limit_bytes=VMEM),
            cost_estimate=pl.CostEstimate(flops=flops, bytes_accessed=nbytes, transcendentals=0),
            name=name,
        )(*args)

    return run


def pack(arrays, plan=None):
    tall = TILE * len(arrays) + (0 if plan is None else EXTRA)
    count = len(arrays)

    def kernel(*refs):
        sources, (out, block, in_sems, out_sems) = refs[:count], refs[-4:]
        loads, stores = [], []
        for i, source in enumerate(sources):
            for at in range(RING):
                n = len(loads)
                loads.append(
                    pltpu.make_async_copy(
                        source.at[0, :, pl.ds(at * GC, GC)], block.at[n], in_sems.at[n]
                    )
                )
                stores.append(
                    pltpu.make_async_copy(
                        block.at[n], out.at[at, pl.ds(i * TILE, TILE)], out_sems.at[n]
                    )
                )
                loads[-1].start()
        if plan is not None:
            for at in range(RING):
                stores.append(
                    pltpu.make_async_copy(
                        refs[count],
                        out.at[at, pl.ds(count * TILE, EXTRA)],
                        out_sems.at[len(stores)],
                    )
                )
                stores[-1].start()
        for load, store in zip(loads, stores):
            load.wait()
            store.start()
        for store in stores:
            store.wait()

    return call(
        kernel,
        f"pack{count}",
        jax.ShapeDtypeStruct((RING, tall, GC), jnp.bfloat16),
        [
            pltpu.VMEM((RING * count, TILE, GC), jnp.bfloat16),
            pltpu.SemaphoreType.DMA((RING * count,)),
            pltpu.SemaphoreType.DMA((RING * (count + 1),)),
        ],
        0,
        RING * tall * GC * 4,
        0,
    )(*arrays, *([] if plan is None else [plan]))


def attend_kernel(first, heads, lists, *refs):
    kv_in, q_in, before, after, out, qb, kvb, ob, in_sems, out_sems = refs
    columns = pl.ds(first * HD, heads * HD)
    base = lax.div(lax.axis_index("ctx"), RING) * RING
    copies = []
    for source, target in (
        (q_in.at[:, pl.ds(0, TILE), columns], qb),
        (kv_in.at[:, :, columns], kvb.at[pl.ds(0, 4)]),
        (before.at[:, :, columns], kvb.at[pl.ds(4, 2)]),
        (after.at[:, :, columns], kvb.at[pl.ds(6, 2)]),
    ):
        copies.append(pltpu.make_async_copy(source, target, in_sems.at[len(copies)]))
        copies[-1].start()
    for copy in copies:
        copy.wait()
    half = TILE // 2

    def tile_of(at, count):
        slots = []
        for s in range(count):
            tile = lists[at, s] - base
            slots.append(tile + jnp.where(tile < 0, 6, jnp.where(tile < RING, 0, 2)))

        def column_of(part, col):
            return jnp.concatenate(
                [kvb[slot, pl.ds(part * TILE, TILE), col] for slot in slots], axis=0
            )

        def score(rows, col):
            scores = lax.dot_general(
                qb[at, rows, col],
                column_of(0, col),
                (((1,), (1,)), ((), ())),
                preferred_element_type=jnp.float32,
            )
            return scores, jnp.max(scores, axis=1, keepdims=True)

        def mix(rows, col, scores, peak):
            probs = jnp.exp2((scores - peak) * FACTOR).astype(jnp.bfloat16)
            ones = jnp.ones((count * TILE, HD), jnp.bfloat16)
            value = jnp.concatenate([column_of(1, col), ones], axis=1)
            total = jnp.dot(probs, value, preferred_element_type=jnp.float32)
            ob[at, rows, col] = (total[:, :HD] / total[:, HD:]).astype(jnp.bfloat16)

        for head in range(heads):
            col = pl.ds(head * HD, HD)
            upper, lower = pl.ds(0, half), pl.ds(half, half)
            first_scores = score(upper, col)
            second_scores = score(lower, col)
            mix(upper, col, *first_scores)
            mix(lower, col, *second_scores)

    def body(at, carry):
        live = lists[at, SLOTS]
        for count in range(1, SLOTS + 1):

            @pl.when(live == count)
            def _():
                tile_of(at, count)

        return carry

    lax.fori_loop(0, RING, body, 0)
    last = pltpu.make_async_copy(ob, out, out_sems.at[0])
    last.start()
    last.wait()


def attend(first, heads, lists, *arrays):
    wide = heads * HD
    return call(
        lambda *refs: attend_kernel(first, heads, *refs),
        f"attend{first}",
        jax.ShapeDtypeStruct((RING, TILE, wide), jnp.bfloat16),
        [
            pltpu.VMEM((RING, TILE, wide), jnp.bfloat16),
            pltpu.VMEM((2 * RING, 2 * TILE, wide), jnp.bfloat16),
            pltpu.VMEM((RING, TILE, wide), jnp.bfloat16),
            pltpu.SemaphoreType.DMA((4,)),
            pltpu.SemaphoreType.DMA((1,)),
        ],
        heads * 5_000_000_000,
        heads * 1_600_000,
        1,
    )(lists, *arrays)


def project(first, heads, part, near, far):
    wide = heads * HD
    deep = RING * wide
    pieces = []
    for shard in range(4):
        low, high = max(shard * 96, first * HD), min(shard * 96 + 96, first * HD + wide)
        if low < high:
            pieces.append((low - first * HD, high - low, shard % 2, shard // 2, low - shard * 96))

    def kernel(*refs):
        part_in, near_in, far_in, *others = refs
        out, rows, weights, result, sems = others
        z_half = lax.rem(lax.div(lax.axis_index("dp"), 2), 2)

        def weight_copies(own):
            copies = []
            for step in range(DOUT // 512):
                col = pl.ds(step * 512, 512)
                for g in range(RING):
                    for to, count, core, half, at in pieces:
                        source = near_in if half == own else far_in
                        copies.append(
                            pltpu.make_async_copy(
                                source.at[pl.ds((2 * g + core) * 96 + at, count), col],
                                weights.at[pl.ds(g * wide + to, count), col],
                                sems.at[len(copies)],
                            )
                        )
            return copies

        waits = weight_copies(0)
        each = RING * len(pieces)
        parts = []
        for g in range(RING):
            copy = pltpu.make_async_copy(
                part_in.at[g], rows.at[:, pl.ds(g * wide, wide)], sems.at[len(waits) + g]
            )
            copy.start()
            parts.append(copy)
        for own in range(2):

            @pl.when(z_half == own)
            def _():
                for copy in weight_copies(own):
                    copy.start()

        for copy in parts:
            copy.wait()
        stores = []
        for step in range(DOUT // 512):
            for copy in waits[step * each : (step + 1) * each]:
                copy.wait()
            col = pl.ds(step * 512, 512)
            product = jnp.dot(rows[...], weights[:, col], preferred_element_type=jnp.float32)
            result[:, col] = product.astype(jnp.bfloat16)
            target = out.at[0, :, col]
            stores.append(pltpu.make_async_copy(result.at[:, col], target, sems.at[len(waits) + step]))
            stores[-1].start()
        for store in stores:
            store.wait()

    shape = jax.ShapeDtypeStruct((1, TILE, DOUT), jnp.bfloat16)
    scratch = [
        pltpu.VMEM((TILE, deep), jnp.bfloat16),
        pltpu.VMEM((deep, DOUT), jnp.bfloat16),
        pltpu.VMEM((TILE, DOUT), jnp.bfloat16),
        pltpu.SemaphoreType.DMA((DOUT // 512 * RING * len(pieces) + RING,)),
    ]
    return call(
        kernel,
        f"project{first}",
        shape,
        scratch,
        2 * TILE * deep * DOUT,
        8_000_000,
        0,
    )(part, near, far)


def per_device(queries, key_rows, value_rows, tile_lists, tile_counts, out_weight):
    groups = [[z * RING + y for y in range(RING)] for z in range(RUNS)]
    pairs = [[x * 4 + high * 2 + core for x in range(4) for core in range(2)] for high in range(2)]

    def exchange(value):
        return lax.all_to_all(value, "ctx", 0, 0, axis_index_groups=groups)

    def gather(value):
        return lax.all_gather(value, "dp", axis=0, tiled=True, axis_index_groups=pairs)

    def halo(value):
        return (
            lax.ppermute(value[2:], "ctx", z_pairs(1)),
            lax.ppermute(value[:2], "ctx", z_pairs(-1)),
        )

    def after(values, done):
        return lax.optimization_barrier((values, done))[0]

    packed = pack((key_rows, value_rows))
    out_weight, queries, tile_lists, tile_counts = after(
        (out_weight, queries, tile_lists, tile_counts), packed
    )
    plan = jnp.concatenate([tile_lists[0], tile_counts], axis=1).astype(jnp.bfloat16)
    plan = jnp.pad(plan, ((0, EXTRA - 1), (0, GC - SLOTS - 1)))
    near = gather(out_weight)
    other = lax.ppermute(out_weight, ("dp", "ctx"), mirror_pairs())
    key_values = exchange(packed)
    packed, key_values, other = lax.optimization_barrier(
        (pack((queries,), plan), key_values, other)
    )
    far = gather(other)
    query = exchange(packed)
    edges = halo(key_values)
    lists = query[:, TILE, :8].astype(jnp.int32)
    query, edges = lax.optimization_barrier((query, edges))
    first, heads = CHUNKS[0]
    mixed = attend(first, heads, lists, key_values, query, *edges)
    return project(first, heads, exchange(mixed), near, far)


def solution(mesh):
    in_specs = (
        P("dp", "ctx", None),
        P("dp", "ctx", None),
        P("dp", "ctx", None),
        P("dp", "ctx", None),
        P("dp", "ctx"),
        P("dp", None),
    )
    out_specs = P("dp", "ctx", None)
    return jax.shard_map(
        per_device, mesh=mesh, in_specs=in_specs, out_specs=out_specs, check_vma=False
    )
```
